512 devices in a mesh: inst: 16 (over y, x), label: 32 (over z, core).
Axes of the slice: x: 4, y: 4, z: 16, core: 2. Of those that a mesh axis runs over, the one named last changes fastest.
Arguments:
- features: bfloat16 [65536, 768], P(('inst', 'label')), may hold values from -6 to 6
- weights: bfloat16 [32768, 768], P('label'), may hold values from -0.21875 to 0.21875
- block_ids: int32 [65536, 16], P(('inst', 'label')), may hold values from 0 to 255, all different within a row; in each aligned block of 128 rows (0 to 127, 128 to 255, ...) at most 16 rows name the same one
- label_codes: int32 [65536, 16], P(('inst', 'label')), may hold values from 0 to 255
- counts: int32 [65536], P(('inst', 'label')), may hold values from 12 to 16
Outputs:
- grad_x: bfloat16 [65536, 768], P(('inst', 'label'))
- grad_w: float32 [32768, 768], P(('label', 'inst'))
- grad_logits: bfloat16 [65536, 16, 128], P(('inst', 'label'))
The draws below stay inside these ranges and needn't reach their ends.
Inputs may be any that keep to these rules, and one draw needn't show every extreme that they name: `block_ids`: each row names 16 different blocks; in the rows of one device no block is named by more than 16 rows, and some block reaches 16. `label_codes`: A code below 128 is the offset of the positive cluster in the slot's block; a code of 128 or more marks a hard negative block. Slots at index counts[n] or beyond are padding.
All inputs are finite; a program needn't handle non-finite values.
Results may differ from the reference program's by a relative error of at most 0.014.
Values may be sent and summed in bfloat16 or wider, within the bound.
No kernel may reach another device: no remote copies, remote signals or barrier semaphores. Data moves between devices by JAX's collectives and lax.ppermute only.
A program may use at most 64 MiB of HBM per device.

```python
import math
import jax
import jax.numpy as jnp
import numpy as np
from jax import lax

D = 768
NB = 256
BS = 128
TOP = 16
TOK_DEV = 128
MOST = 16
TOKENS = 65536
N_INST = 16
N_LABEL = 32


def with_ends(array, rng, smallest, high):
    place = [jax.random.randint(jax.random.fold_in(rng, axis), (), 0, length) for axis, length in enumerate(array.shape)]
    widest = array.shape.index(max(array.shape))
    neighbour = place[:widest] + [(place[widest] + 1) % array.shape[widest]] + place[widest + 1:]
    return array.at[tuple(place)].set(smallest).at[tuple(neighbour)].set(high)


def block_scale(own_key, extent, split, least, high):
    def one(dim, blocks):
        draws = jax.random.uniform(jax.random.fold_in(jax.random.fold_in(own_key, 6), dim), (blocks,), jnp.float32, least / len(split), high / len(split))
        return jnp.repeat(jnp.exp(draws), extent[dim] // blocks).reshape((-1,) + (1,) * (len(extent) - dim - 1))

    gain = one(*split[0])
    for cut in split[1:]:
        gain = gain * one(*cut)
    return gain


def shared_out(stream_key, own, number, rows, amount, top, most, skew):
    order = jax.random.permutation(stream_key, amount)
    crowded, common = shares(amount, rows * top, most, skew, True), shares(amount, rows * top, most, skew, False)
    places = jnp.arange(amount)

    def named(tallies, rotation):
        used = int((tallies > 0).sum())
        fixed = max(1, used // 4)
        moved = fixed + (places - fixed + rotation * (used - fixed)) % max(1, amount - fixed)
        return jnp.zeros((amount,), jnp.int32).at[order[jnp.where(places < fixed, places, moved)]].set(jnp.asarray(tallies, jnp.int32))

    tallies = jnp.where(number % 4 == 0, named(crowded, number // 4), named(common, number - number // 4 - 1))
    mixed = jax.random.permutation(jax.random.fold_in(own, 3), amount)
    source_of, taker = mixed[0:amount // 2 * 2:2], mixed[1:amount // 2 * 2:2]
    margin = jnp.minimum(tallies[source_of] - 1, most - tallies[taker]) // 2
    margin = jnp.where((source_of == order[0]) | (taker == order[0]) | (tallies[taker] == 0), 0, jnp.maximum(margin, 0))
    moved = jax.random.randint(jax.random.fold_in(own, 4), (amount // 2,), 0, 1 << 20) % (margin + 1)
    tallies = tallies.at[source_of].add(-moved).at[taker].add(moved)
    labels = jnp.searchsorted(jnp.cumsum(tallies), jnp.arange(rows * top), side="right").astype(jnp.int32)
    listing = labels.reshape(top, rows).T
    listing = listing[jax.random.permutation(jax.random.fold_in(own, 1), rows)]
    rotation = jax.random.randint(jax.random.fold_in(own, 2), (rows, 1), 0, top)
    return jnp.take_along_axis(listing, (jnp.arange(top)[None, :] + rotation) % top, axis=1)


def shares(count, total, most, slope, full):
    weights = [(1 << 20) // math.isqrt(rank ** slope) + 1 for rank in range(1, count + 1)]
    largest = most if full else min(most, max(-(-total // count), total * weights[0] // sum(weights)))
    least = 1 if total - largest >= count - 1 else 0
    given, spare = [largest] + [least] * (count - 1), total - largest - least * (count - 1)
    while spare > 0:
        candidates = [i for i in range(1, count) if given[i] < largest] or [i for i in range(1, count) if given[i] < most]
        whole, remaining = sum([weights[i] for i in candidates]), spare
        for i in candidates:
            extra = min(most - given[i], max(1, remaining * weights[i] // whole), spare)
            given[i] = given[i] + extra
            spare = spare - extra
    return np.array(given)


def bell_draw(stream_key, dims, deviation, limit, cuts=(), kind=jnp.bfloat16):
    array = jax.random.normal(stream_key, dims, jnp.float32) * deviation
    if len(cuts) > 0:
        array = block_scale(stream_key, dims, cuts, -0.22, 0.18) * array
    return jnp.clip(array, min=-limit, max=limit).astype(kind)


def setup_inputs(seed: int = 0) -> dict:
    arg_keys = jax.random.split(jax.random.key(seed), 6)
    features = bell_draw(arg_keys[0], (TOKENS, D), 1.0, 6.0, ((0, 512),))
    weights = bell_draw(arg_keys[1], (NB * BS, D), D ** -0.5, 0.21875, ((0, 32),))
    block_ids_keys = jax.random.split(jax.random.fold_in(arg_keys[2], 1), TOKENS // TOK_DEV)
    block_ids_turns = jax.random.permutation(jax.random.fold_in(arg_keys[2], 3), TOKENS // TOK_DEV)
    block_ids = jax.vmap(lambda own, number: shared_out(jax.random.fold_in(arg_keys[2], 2), own, number, TOK_DEV, NB, TOP, MOST, 2))(block_ids_keys, block_ids_turns).reshape((TOKENS, TOP))
    label_codes = with_ends(jax.random.randint(arg_keys[3], (TOKENS, TOP), 0, 2 * BS), jax.random.fold_in(arg_keys[3], 1), 0, (2 * BS) - 1).astype(jnp.int32)
    counts = with_ends(jax.random.randint(arg_keys[4], (TOKENS,), 12, TOP + 1), jax.random.fold_in(arg_keys[4], 1), 12, TOP).astype(jnp.int32)
    return {"features": features, "weights": weights, "block_ids": block_ids, "label_codes": label_codes, "counts": counts}


def bucket_slots(flat_ids):
    one_hot = (flat_ids[:, None] == jnp.arange(NB, dtype=jnp.int32)[None, :]).astype(jnp.int32)
    rank_within = jnp.sum((jnp.cumsum(one_hot, axis=0) - one_hot) * one_hot, axis=1)
    return flat_ids * MOST + rank_within


def reference(features, weights, block_ids, label_codes, counts):
    device_count = N_INST * N_LABEL
    pair_count = TOK_DEV * TOP
    spare_pair = device_count * pair_count
    slot_index = lax.map(bucket_slots, block_ids.reshape(device_count, pair_count))
    device_base = (jnp.arange(device_count, dtype=jnp.int32) * (NB * MOST))[:, None]
    flat_slot = (device_base + slot_index).reshape(-1)
    pair_numbers = jnp.arange(spare_pair, dtype=jnp.int32)
    bucket_table = jnp.full((device_count * NB * MOST,), spare_pair, jnp.int32).at[flat_slot].set(pair_numbers)
    bucket_table = bucket_table.reshape(device_count, NB, MOST).transpose(1, 0, 2).reshape(NB, device_count * MOST)
    padded_rows = jnp.concatenate([features, jnp.zeros((1, D), features.dtype)], 0)
    slot_numbers = jnp.arange(TOP, dtype=jnp.int32)[None, :]
    pair_codes = jnp.where(slot_numbers < counts[:, None], label_codes, -1).reshape(-1)
    pair_codes = jnp.concatenate([pair_codes, jnp.full((1,), -1, jnp.int32)])
    pair_rows = jnp.concatenate([pair_numbers // TOP, jnp.full((1,), TOKENS, jnp.int32)])
    block_weights = weights.reshape(NB, BS, D)
    offsets = jnp.arange(BS, dtype=jnp.int32)

    def per_block(running, inputs):
        grad_rows, grad_table = running
        entries, block_weight = inputs
        row_index = pair_rows[entries]
        chosen = padded_rows[row_index]
        slot_code = pair_codes[entries]
        logits = jnp.dot(chosen, block_weight.T, preferred_element_type=jnp.float32)
        target = (slot_code[:, None] == offsets[None, :]).astype(jnp.float32)
        alive_mask = (slot_code >= 0).astype(jnp.float32)[:, None]
        logit_grad = (alive_mask * (jax.nn.sigmoid(logits) - target)).astype(jnp.bfloat16)
        slot_grads = jnp.dot(logit_grad, block_weight, preferred_element_type=jnp.float32).astype(jnp.bfloat16)
        grad_rows = grad_rows.at[row_index].add(slot_grads.astype(jnp.float32))
        grad_table = grad_table.at[entries].set(logit_grad)
        group_grads = jnp.einsum("gmc,gmd->gcd",
                                 logit_grad.reshape(N_INST, -1, BS).astype(jnp.float32),
                                 chosen.reshape(N_INST, -1, D).astype(jnp.float32))
        rounded = lax.optimization_barrier(group_grads.astype(jnp.bfloat16))
        weight_sum = jnp.sum(rounded.astype(jnp.float32), axis=0)
        return (grad_rows, grad_table), weight_sum

    start_rows = jnp.zeros((TOKENS + 1, D), jnp.float32)
    start_table = jnp.zeros((spare_pair + 1, BS), jnp.bfloat16)
    (grad_rows, grad_table), weight_sums = lax.scan(per_block, (start_rows, start_table), (bucket_table, block_weights))
    grad_x = grad_rows[:TOKENS].astype(jnp.bfloat16)
    grad_w = weight_sums.reshape(NB * BS, D)
    grad_logits = grad_table[:spare_pair].reshape(TOKENS, TOP, BS)
    return grad_x, grad_w, grad_logits
```

```python
import functools

import jax
import jax.numpy as jnp
from jax import lax
from jax.experimental import pallas as pl
from jax.experimental.pallas import tpu as pltpu
from jax.sharding import Mesh
from jax.sharding import PartitionSpec as P

BS = 128
MOST = 16
TOP = 16
ROWS = 128
META = 16
D = 768
Z = 16
HALF = BS // 2
COLS = Z * HALF
STEP = 4
PLANE = ("y", "x")
NT = (((1,), (1,)), ((), ()))
F32 = jnp.float32
BF16 = jnp.bfloat16


def expert_body(first, meta, x_ref, w_ref, wt_ref, *refs):
    if first:
        out_ref, gw_ref, acc, grad = refs
    else:
        gw_in, out_ref, gw_ref, acc, grad = refs
    step = pl.program_id(0)
    base = meta[0].astype(F32)
    offset = (meta[1] * HALF + 2).astype(F32)
    n = STEP * ROWS
    x = x_ref[:, :ROWS, :].reshape(n, D)

    @pl.when(step == 0)
    def _():
        if first:
            acc[...] = jnp.zeros_like(acc)
        else:
            acc[...] = gw_in[...]

    wanted = lax.broadcasted_iota(jnp.int32, (Z, ROWS), 0).astype(F32) * 16.0 + base
    before = (
        lax.broadcasted_iota(jnp.int32, (ROWS, ROWS), 0)
        < lax.broadcasted_iota(jnp.int32, (ROWS, ROWS), 1)
    ).astype(F32).astype(BF16)
    entries, ranks = [], []
    for d in range(STEP):
        ids = x_ref[d, ROWS : ROWS + TOP, :ROWS].astype(F32)
        codes = x_ref[d, ROWS : ROWS + TOP, ROWS : 2 * ROWS].astype(F32)
        entry = jnp.zeros((Z, ROWS), F32)
        for k in range(TOP):
            entry = entry + jnp.where(ids[k : k + 1, :] == wanted, codes[k : k + 1, :], 0.0)
        named = entry > 0.0
        rank = jnp.dot(
            jnp.where(named, 1.0, 0.0).astype(BF16), before, preferred_element_type=F32
        )
        entries.append(entry)
        ranks.append(jnp.where(named, rank, -1.0))
    entry = jnp.concatenate(entries, axis=1)
    place = lax.broadcasted_iota(jnp.int32, (HALF, n), 0).astype(F32) + offset
    part = 4 * HALF
    for q in range(COLS // part):
        logits = lax.dot_general(
            w_ref[q * part : (q + 1) * part, :], x, NT, preferred_element_type=F32
        )
        for s in range(4):
            z = 4 * q + s
            code = jnp.broadcast_to(entry[z : z + 1, :], (HALF, n))
            own = logits[s * HALF : (s + 1) * HALF, :]
            sig = 0.5 * jnp.tanh(0.5 * own) + 0.5
            value = jnp.where(code >= 2.0, jnp.where(code == place, sig - 1.0, sig), 0.0)
            grad[z * HALF : (z + 1) * HALF, :] = value.astype(BF16)
    for q in range(COLS // part):
        acc[q * part : (q + 1) * part, :] += jnp.dot(
            grad[q * part : (q + 1) * part, :], x, preferred_element_type=F32
        )
    for q in range(D // 256):
        back = jnp.dot(
            wt_ref[q * 256 : (q + 1) * 256, :], grad[...], preferred_element_type=F32
        ).astype(BF16)
        for d in range(STEP):
            out_ref[d, q * 256 : (q + 1) * 256, :] = back[:, d * ROWS : (d + 1) * ROWS]
    slot = lax.broadcasted_iota(jnp.int32, (MOST, ROWS), 0).astype(F32)
    lane = lax.broadcasted_iota(jnp.int32, (HALF, ROWS), 1) // MOST
    for d in range(STEP):
        for hh in range(2):
            pick = jnp.concatenate(
                [
                    jnp.where(
                        jnp.broadcast_to(ranks[d][z : z + 1, :], (MOST, ROWS)) == slot, 1.0, 0.0
                    )
                    for z in range(8 * hh, 8 * hh + 8)
                ],
                axis=0,
            ).astype(BF16)
            mixed = lax.dot_general(
                grad[hh * 512 : (hh + 1) * 512, d * ROWS : (d + 1) * ROWS],
                pick,
                NT,
                preferred_element_type=F32,
            )
            packed = jnp.zeros((HALF, ROWS), F32)
            for z in range(8):
                packed = jnp.where(lane == z, mixed[z * HALF : (z + 1) * HALF, :], packed)
            out_ref[d, D + hh * HALF : D + (hh + 1) * HALF, :] = packed.astype(BF16)

    @pl.when(step == pl.num_programs(0) - 1)
    def _():
        gw_ref[...] = acc[...].astype(gw_ref.dtype)


def expert(meta, rows, w, wt, total=None):
    first = total is None
    count = rows.shape[0]
    whole = lambda shape: pl.BlockSpec(shape, lambda i, m: (0,) * len(shape))
    in_specs = [
        pl.BlockSpec((STEP, ROWS + META, D), lambda i, m: (i, 0, 0)),
        whole((COLS, D)),
        whole((D, COLS)),
    ]
    args = [meta, rows, w, wt]
    if not first:
        in_specs.append(whole((COLS, D)))
        args.append(total)
    flops = 3 * 2 * count * ROWS * COLS * D
    return pl.pallas_call(
        functools.partial(expert_body, first),
        grid_spec=pltpu.PrefetchScalarGridSpec(
            num_scalar_prefetch=1,
            grid=(count // STEP,),
            in_specs=in_specs,
            out_specs=[
                pl.BlockSpec((STEP, D + BS, ROWS), lambda i, m: (i, 0, 0)),
                whole((COLS, D)),
            ],
            scratch_shapes=[
                pltpu.VMEM((COLS, D), F32),
                pltpu.VMEM((COLS, STEP * ROWS), BF16),
            ],
        ),
        out_shape=[
            jax.ShapeDtypeStruct((count, D + BS, ROWS), BF16),
            jax.ShapeDtypeStruct((COLS, D), F32 if first else BF16),
        ],
        compiler_params=pltpu.CompilerParams(vmem_limit_bytes=48 * 2**20),
        cost_estimate=pl.CostEstimate(
            flops=flops, bytes_accessed=20 * 2**20, transcendentals=count * ROWS * COLS
        ),
    )(*args)


def unpack_body(key_ref, got_ref, out_ref):
    key = key_ref[...]
    lane = lax.broadcasted_iota(jnp.int32, (1, 2 * ROWS), 1)
    total = jnp.zeros(out_ref.shape, F32)
    for owner in range(8):
        for other in range(2):
            chunk = owner * 2 + other
            base = D + other * BS
            table = jnp.concatenate(
                [
                    jnp.concatenate(
                        [
                            got_ref[2 * owner + h, base + hh * HALF : base + (hh + 1) * HALF, :]
                            for hh in range(2)
                        ],
                        axis=1,
                    )
                    for h in range(2)
                ],
                axis=0,
            )
            pick = jnp.where(key == lane + chunk * 2 * ROWS, 1.0, 0.0).astype(BF16)
            total += lax.dot_general(pick, table, NT, preferred_element_type=F32)
    out_ref[...] = total.astype(BF16)


def unpack(key, got):
    pairs = key.shape[0]
    block = 512
    return pl.pallas_call(
        unpack_body,
        grid=(pairs // block,),
        in_specs=[
            pl.BlockSpec((block, 2 * ROWS), lambda i: (i, 0)),
            pl.BlockSpec(got.shape, lambda i: (0, 0, 0)),
        ],
        out_specs=pl.BlockSpec((block, BS), lambda i: (i, 0)),
        out_shape=jax.ShapeDtypeStruct((pairs, BS), BF16),
        compiler_params=pltpu.CompilerParams(vmem_limit_bytes=48 * 2**20),
        cost_estimate=pl.CostEstimate(
            flops=2 * pairs * 4096 * BS, bytes_accessed=8 * 2**20, transcendentals=0
        ),
    )(key, got)


def shards(features, weights, block_ids, label_codes, counts):
    inst = lax.axis_index(PLANE)
    core = lax.axis_index("core")
    meta = jnp.stack([8 * core + inst // 2, inst % 2]).astype(jnp.int32)
    mine = lax.dynamic_slice_in_dim(weights, inst * HALF, HALF, 0)
    w = lax.all_gather(mine, "z").reshape(COLS, D)
    wt = w.T

    alive = jnp.arange(TOP, dtype=jnp.int32)[None, :] < counts[:, None]
    code = jnp.where(alive, jnp.minimum(label_codes, BS) + 2, 1)
    slots = jnp.concatenate([block_ids.T, code.T], axis=1).astype(BF16)
    slots = jnp.pad(slots, ((0, 0), (0, D - 2 * ROWS)))
    sent = jnp.concatenate([features, slots], axis=0)
    own = lax.all_gather(sent, PLANE)
    swap = [(0, 1), (1, 0)]
    other = lax.ppermute(own, "core", swap)
    own_out, total = expert(meta, own, w, wt)
    other_out, total = expert(meta, other, w, wt, total)
    back = lax.ppermute(other_out, "core", swap)
    grad_w = lax.psum_scatter(
        total.reshape(Z, HALF, D), "z", scatter_dimension=0, tiled=False
    ).astype(F32)
    sums = (own_out[:, :D].astype(F32) + back[:, :D].astype(F32)).astype(BF16)
    payload = jnp.concatenate([sums, own_out[:, D:], back[:, D:]], axis=1)
    got = lax.all_to_all(payload, PLANE, split_axis=0, concat_axis=0, tiled=True)
    grad_x = jnp.sum(got[:, :D], axis=0, dtype=F32).T.astype(BF16)

    blocks = jnp.arange(256, dtype=jnp.int32)
    named = (block_ids[:, :, None] == blocks).any(axis=1).astype(BF16)
    order = jnp.arange(ROWS, dtype=jnp.int32)
    before = (order[None, :] < order[:, None]).astype(BF16)
    rank = jnp.dot(before, named, preferred_element_type=F32)
    rank = jnp.sum(jnp.where(block_ids[:, :, None] == blocks, rank[:, None, :], 0.0), axis=2)
    rank = rank.astype(jnp.int32)
    row = block_ids // 16
    owner = block_ids % 16
    crossed = (owner // 8) ^ core
    key = (((owner % 8) * 2 + crossed) * 2 + row // 8) * ROWS + (row % 8) * MOST + rank
    key = jnp.broadcast_to(key.reshape(-1, 1), (ROWS * TOP, 2 * ROWS))
    grad_logits = unpack(key, got).reshape(ROWS, TOP, BS)
    return (grad_x, grad_w, grad_logits)


def solution(mesh):
    mesh = Mesh(mesh.devices.reshape(4, 4, Z, 2), ("y", "x", "z", "core"))
    everywhere = ("y", "x", "z", "core")
    in_specs = (
        P(everywhere, None),
        P(("z", "core"), None),
        P(everywhere, None),
        P(everywhere, None),
        P(everywhere),
    )
    out_specs = (
        P(everywhere, None),
        P(("z", "core", "y", "x"), None),
        P(everywhere, None, None),
    )
    return jax.shard_map(shards, mesh=mesh, in_specs=in_specs, out_specs=out_specs, check_vma=False)
```

```python
import functools

import jax
import jax.numpy as jnp
from jax import lax
from jax.experimental import pallas as pl
from jax.experimental.pallas import tpu as pltpu
from jax.sharding import Mesh
from jax.sharding import PartitionSpec as P

BS = 128
MOST = 16
TOP = 16
ROWS = 128
META = 16
D = 768
Z = 16
HALF = BS // 2
COLS = Z * HALF
STEP = 4
PLANE = ("y", "x")
NT = (((1,), (1,)), ((), ()))
F32 = jnp.float32
BF16 = jnp.bfloat16
VMEM = 48 * 2**20


def expert_body(meta, x_ref, w_ref, grad, pack_ref):
    base = meta[0].astype(F32)
    offset = (meta[1] * HALF + 2).astype(F32)
    n = STEP * ROWS
    x = x_ref[:, :ROWS, :].reshape(n, D)
    chunk = lax.rem(lax.broadcasted_iota(jnp.int32, (Z, ROWS), 0) + meta[2], Z)
    wanted = chunk.astype(F32) * 16.0 + base
    before = (
        lax.broadcasted_iota(jnp.int32, (ROWS, ROWS), 0)
        < lax.broadcasted_iota(jnp.int32, (ROWS, ROWS), 1)
    ).astype(F32).astype(BF16)
    entries, ranks = [], []
    for d in range(STEP):
        ids = x_ref[d, ROWS : ROWS + TOP, :ROWS].astype(F32)
        codes = x_ref[d, ROWS : ROWS + TOP, ROWS : 2 * ROWS].astype(F32)
        entry = jnp.zeros((Z, ROWS), F32)
        for k in range(TOP):
            entry = entry + jnp.where(ids[k : k + 1, :] == wanted, codes[k : k + 1, :], 0.0)
        named = entry > 0.0
        rank = jnp.dot(
            jnp.where(named, 1.0, 0.0).astype(BF16), before, preferred_element_type=F32
        )
        entries.append(entry)
        ranks.append(jnp.where(named, rank, -1.0))
    entry = jnp.concatenate(entries, axis=1)
    place = lax.broadcasted_iota(jnp.int32, (HALF, n), 0).astype(F32) + offset
    part = 4 * HALF
    for q in range(COLS // part):
        logits = lax.dot_general(
            w_ref[q * part : (q + 1) * part, :], x, NT, preferred_element_type=F32
        )
        for s in range(4):
            z = 4 * q + s
            code = jnp.broadcast_to(entry[z : z + 1, :], (HALF, n))
            own = logits[s * HALF : (s + 1) * HALF, :]
            sig = 0.5 * jnp.tanh(0.5 * own) + 0.5
            value = jnp.where(code >= 2.0, jnp.where(code == place, sig - 1.0, sig), 0.0)
            grad[z * HALF : (z + 1) * HALF, :] = value.astype(BF16)
    slot = lax.broadcasted_iota(jnp.int32, (MOST, ROWS), 0).astype(F32)
    lane = lax.broadcasted_iota(jnp.int32, (HALF, ROWS), 1) // MOST
    for d in range(STEP):
        for hh in range(2):
            pick = jnp.concatenate(
                [
                    jnp.where(
                        jnp.broadcast_to(ranks[d][z : z + 1, :], (MOST, ROWS)) == slot, 1.0, 0.0
                    )
                    for z in range(8 * hh, 8 * hh + 8)
                ],
                axis=0,
            ).astype(BF16)
            mixed = lax.dot_general(
                grad[hh * 512 : (hh + 1) * 512, d * ROWS : (d + 1) * ROWS],
                pick,
                NT,
                preferred_element_type=F32,
            )
            packed = jnp.zeros((HALF, ROWS), F32)
            for z in range(8):
                packed = jnp.where(lane == z, mixed[z * HALF : (z + 1) * HALF, :], packed)
            pack_ref[d, hh * HALF : (hh + 1) * HALF, :] = packed.astype(BF16)


def expert(meta, rows, w):
    count = rows.shape[0]
    return pl.pallas_call(
        expert_body,
        grid_spec=pltpu.PrefetchScalarGridSpec(
            num_scalar_prefetch=1,
            grid=(count // STEP,),
            in_specs=[
                pl.BlockSpec((STEP, ROWS + META, D), lambda i, m: (i, 0, 0)),
                pl.BlockSpec((COLS, D), lambda i, m: (0, 0)),
            ],
            out_specs=[
                pl.BlockSpec((COLS, STEP * ROWS), lambda i, m: (0, i)),
                pl.BlockSpec((STEP, BS, ROWS), lambda i, m: (i, 0, 0)),
            ],
        ),
        out_shape=[
            jax.ShapeDtypeStruct((COLS, count * ROWS), BF16),
            jax.ShapeDtypeStruct((count, BS, ROWS), BF16),
        ],
        compiler_params=pltpu.CompilerParams(vmem_limit_bytes=VMEM),
        cost_estimate=pl.CostEstimate(
            flops=2 * count * ROWS * COLS * D,
            bytes_accessed=10 * 2**20,
            transcendentals=count * ROWS * COLS,
        ),
    )(meta, rows, w)


def weight_body(ga_ref, xa_ref, gb_ref, xb_ref, out_ref, acc):
    step, half = pl.program_id(0), pl.num_programs(0) // 2

    def add(g_ref, x_ref):
        x = x_ref[:, :ROWS, :].reshape(-1, D)
        for q in range(4):
            rows = slice(q * 256, (q + 1) * 256)
            acc[rows, :] += jnp.dot(g_ref[rows, :], x, preferred_element_type=F32)

    @pl.when(step == 0)
    def _():
        acc[...] = jnp.zeros_like(acc)

    @pl.when(step < half)
    def _():
        add(ga_ref, xa_ref)

    @pl.when(step >= half)
    def _():
        add(gb_ref, xb_ref)

    @pl.when(step == pl.num_programs(0) - 1)
    def _():
        out_ref[...] = acc[...].astype(BF16)


def weight_grad(ga, xa, gb, xb):
    count, block = xa.shape[0], 8
    half = count // block
    low = lambda i: jnp.minimum(i, half - 1)
    high = lambda i: jnp.maximum(i - half, 0)
    return pl.pallas_call(
        weight_body,
        grid=(2 * half,),
        in_specs=[
            pl.BlockSpec((COLS, block * ROWS), lambda i: (0, low(i))),
            pl.BlockSpec((block, ROWS + META, D), lambda i: (low(i), 0, 0)),
            pl.BlockSpec((COLS, block * ROWS), lambda i: (0, high(i))),
            pl.BlockSpec((block, ROWS + META, D), lambda i: (high(i), 0, 0)),
        ],
        out_specs=pl.BlockSpec((COLS, D), lambda i: (0, 0)),
        out_shape=jax.ShapeDtypeStruct((COLS, D), BF16),
        scratch_shapes=[pltpu.VMEM((COLS, D), F32)],
        compiler_params=pltpu.CompilerParams(vmem_limit_bytes=VMEM),
        cost_estimate=pl.CostEstimate(
            flops=4 * count * ROWS * COLS * D, bytes_accessed=18 * 2**20, transcendentals=0
        ),
    )(ga, xa, gb, xb)


def row_body(wt_ref, g_ref, out_ref):
    for q in range(D // 256):
        back = jnp.dot(
            wt_ref[q * 256 : (q + 1) * 256, :], g_ref[...], preferred_element_type=F32
        ).astype(BF16)
        for d in range(STEP):
            out_ref[d, q * 256 : (q + 1) * 256, :] = back[:, d * ROWS : (d + 1) * ROWS]


def row_grad(wt, g):
    count = g.shape[1] // ROWS
    return pl.pallas_call(
        row_body,
        grid=(count // STEP,),
        in_specs=[
            pl.BlockSpec((D, COLS), lambda i: (0, 0)),
            pl.BlockSpec((COLS, STEP * ROWS), lambda i: (0, i)),
        ],
        out_specs=pl.BlockSpec((STEP, D, ROWS), lambda i: (i, 0, 0)),
        out_shape=jax.ShapeDtypeStruct((count, D, ROWS), BF16),
        compiler_params=pltpu.CompilerParams(vmem_limit_bytes=VMEM),
        cost_estimate=pl.CostEstimate(
            flops=2 * count * ROWS * COLS * D, bytes_accessed=9 * 2**20, transcendentals=0
        ),
    )(wt, g)


def shift(x, k):
    return lax.ppermute(x, "z", [(s, (s - k) % Z) for s in range(Z)])


def gather_z(mine):
    ahead, behind, across = shift(mine, 4), shift(mine, -4), shift(mine, 8)
    every = jnp.stack([mine, ahead, across, behind])
    half = HALF // 2
    one, last = shift(every, 1), shift(every, -1)
    low, high = shift(every[:, :half], 2), shift(every[:, half:], -2)
    two = jnp.concatenate([low, jnp.roll(high, -1, axis=0)], axis=1)
    parts = [every, one, two, jnp.roll(last, -1, axis=0)]
    return jnp.stack(parts, axis=1).reshape((Z,) + mine.shape)


def reduce_z(total):
    half = HALF // 2
    total = total.reshape(4, 4, HALF, D)
    last = jnp.roll(total[:, 3], 1, axis=0)
    two = total[:, 2]
    one, last = shift(total[:, 1], -1), shift(last, 1)
    low, high = shift(two[:, :half], -2), shift(jnp.roll(two[:, half:], 1, axis=0), 2)
    every = total[:, 0].astype(F32) + one.astype(F32) + last.astype(F32)
    every = every + jnp.concatenate([low, high], axis=1).astype(F32)
    sent = every[1:].astype(BF16)
    got = [shift(sent[0], -4), shift(sent[1], 8), shift(sent[2], 4)]
    return every[0] + got[0].astype(F32) + got[1].astype(F32) + got[2].astype(F32)


def unpack_body(key_ref, got_ref, out_ref):
    key = key_ref[...]
    lane = lax.broadcasted_iota(jnp.int32, (1, 2 * ROWS), 1)
    total = jnp.zeros(out_ref.shape, F32)
    for owner in range(8):
        for other in range(2):
            chunk = owner * 2 + other
            base = other * BS
            table = jnp.concatenate(
                [
                    jnp.concatenate(
                        [
                            got_ref[2 * owner + h, base + hh * HALF : base + (hh + 1) * HALF, :]
                            for hh in range(2)
                        ],
                        axis=1,
                    )
                    for h in range(2)
                ],
                axis=0,
            )
            pick = jnp.where(key == lane + chunk * 2 * ROWS, 1.0, 0.0).astype(BF16)
            total += lax.dot_general(pick, table, NT, preferred_element_type=F32)
    out_ref[...] = total.astype(BF16)


def unpack(key, got):
    pairs = key.shape[0]
    block = 512
    return pl.pallas_call(
        unpack_body,
        grid=(pairs // block,),
        in_specs=[
            pl.BlockSpec((block, 2 * ROWS), lambda i: (i, 0)),
            pl.BlockSpec(got.shape, lambda i: (0, 0, 0)),
        ],
        out_specs=pl.BlockSpec((block, BS), lambda i: (i, 0)),
        out_shape=jax.ShapeDtypeStruct((pairs, BS), BF16),
        compiler_params=pltpu.CompilerParams(vmem_limit_bytes=VMEM),
        cost_estimate=pl.CostEstimate(
            flops=2 * pairs * 4096 * BS, bytes_accessed=8 * 2**20, transcendentals=0
        ),
    )(key, got)


def shards(features, weights, block_ids, label_codes, counts):
    inst = lax.axis_index(PLANE)
    core = lax.axis_index("core")
    depth = lax.axis_index("z")
    meta = jnp.stack([8 * core + inst // 2, inst % 2, depth]).astype(jnp.int32)
    mine = lax.dynamic_slice_in_dim(weights, inst * HALF, HALF, 0)
    w = gather_z(mine).reshape(COLS, D)
    wt = w.T

    alive = jnp.arange(TOP, dtype=jnp.int32)[None, :] < counts[:, None]
    code = jnp.where(alive, jnp.minimum(label_codes, BS) + 2, 1)
    slots = jnp.concatenate([block_ids.T, code.T], axis=1).astype(BF16)
    slots = jnp.pad(slots, ((0, 0), (0, D - 2 * ROWS)))
    sent = jnp.concatenate([features, slots], axis=0)
    copies = jnp.broadcast_to(sent[None], (Z,) + sent.shape)
    own = lax.all_to_all(copies, PLANE, split_axis=0, concat_axis=0, tiled=True)
    swap = [(0, 1), (1, 0)]
    other = lax.ppermute(own, "core", swap)
    own_grad, own_pack = expert(meta, own, w)
    other_grad, other_pack = expert(meta, other, w)
    total = weight_grad(own_grad, own, other_grad, other)
    back_pack = lax.ppermute(other_pack, "core", swap)
    packs = jnp.concatenate([own_pack, back_pack], axis=1)
    got = lax.all_to_all(packs, PLANE, split_axis=0, concat_axis=0, tiled=True)
    total, other_grad, own_grad = lax.optimization_barrier((total, other_grad, own_grad))
    grad_w = reduce_z(total)
    back_rows = lax.ppermute(row_grad(wt, other_grad), "core", swap)
    sums = (row_grad(wt, own_grad).astype(F32) + back_rows.astype(F32)).astype(BF16)
    got_rows = lax.all_to_all(sums, PLANE, split_axis=0, concat_axis=0, tiled=True)
    grad_x = jnp.sum(got_rows, axis=0, dtype=F32).T.astype(BF16)

    blocks = jnp.arange(256, dtype=jnp.int32)
    named = (block_ids[:, :, None] == blocks).any(axis=1).astype(BF16)
    order = jnp.arange(ROWS, dtype=jnp.int32)
    before = (order[None, :] < order[:, None]).astype(BF16)
    rank = jnp.dot(before, named, preferred_element_type=F32)
    rank = jnp.sum(jnp.where(block_ids[:, :, None] == blocks, rank[:, None, :], 0.0), axis=2)
    rank = rank.astype(jnp.int32)
    row = (block_ids // 16 - depth) % Z
    owner = block_ids % 16
    crossed = (owner // 8) ^ core
    key = (((owner % 8) * 2 + crossed) * 2 + row // 8) * ROWS + (row % 8) * MOST + rank
    key = jnp.broadcast_to(key.reshape(-1, 1), (ROWS * TOP, 2 * ROWS))
    grad_logits = unpack(key, got).reshape(ROWS, TOP, BS)
    return (grad_x, grad_w, grad_logits)


def solution(mesh):
    mesh = Mesh(mesh.devices.reshape(4, 4, Z, 2), ("y", "x", "z", "core"))
    everywhere = ("y", "x", "z", "core")
    in_specs = (
        P(everywhere, None),
        P(("z", "core"), None),
        P(everywhere, None),
        P(everywhere, None),
        P(everywhere),
    )
    out_specs = (
        P(everywhere, None),
        P(("z", "core", "y", "x"), None),
        P(everywhere, None, None),
    )
    return jax.shard_map(shards, mesh=mesh, in_specs=in_specs, out_specs=out_specs, check_vma=False)
```

```python
import functools

import jax
import jax.numpy as jnp
from jax import lax
from jax.experimental import pallas as pl
from jax.experimental.pallas import tpu as pltpu
from jax.sharding import Mesh
from jax.sharding import PartitionSpec as P

BS = 128
MOST = 16
TOP = 16
ROWS = 128
META = 16
D = 768
Z = 16
HALF = BS // 2
COLS = Z * HALF
STEP = 4
PLANE = ("y", "x")
NT = (((1,), (1,)), ((), ()))
F32 = jnp.float32
BF16 = jnp.bfloat16
VMEM = 48 * 2**20


def expert_body(meta, x_ref, w_ref, grad, pack_ref):
    base = meta[0].astype(F32)
    offset = (meta[1] * HALF + 2).astype(F32)
    n = STEP * ROWS
    x = x_ref[:, :ROWS, :].reshape(n, D)
    wanted = lax.broadcasted_iota(jnp.int32, (Z, ROWS), 0).astype(F32) * 16.0 + base
    before = (
        lax.broadcasted_iota(jnp.int32, (ROWS, ROWS), 0)
        < lax.broadcasted_iota(jnp.int32, (ROWS, ROWS), 1)
    ).astype(F32).astype(BF16)
    entries, ranks = [], []
    for d in range(STEP):
        ids = x_ref[d, ROWS : ROWS + TOP, :ROWS].astype(F32)
        codes = x_ref[d, ROWS : ROWS + TOP, ROWS : 2 * ROWS].astype(F32)
        entry = jnp.zeros((Z, ROWS), F32)
        for k in range(TOP):
            entry = entry + jnp.where(ids[k : k + 1, :] == wanted, codes[k : k + 1, :], 0.0)
        named = entry > 0.0
        rank = jnp.dot(
            jnp.where(named, 1.0, 0.0).astype(BF16), before, preferred_element_type=F32
        )
        entries.append(entry)
        ranks.append(jnp.where(named, rank, -1.0))
    entry = jnp.concatenate(entries, axis=1)
    gain = jnp.where(entry >= 2.0, 0.5, 0.0)
    place = lax.broadcasted_iota(jnp.int32, (HALF, n), 0).astype(F32) + offset
    part = 4 * HALF
    for q in range(COLS // part):
        logits = lax.dot_general(
            w_ref[q * part : (q + 1) * part, :], x, NT, preferred_element_type=F32
        )
        for s in range(4):
            z = 4 * q + s
            code = jnp.broadcast_to(entry[z : z + 1, :], (HALF, n))
            own = logits[s * HALF : (s + 1) * HALF, :]
            sig = (jnp.tanh(0.5 * own) + 1.0) * jnp.broadcast_to(gain[z : z + 1, :], (HALF, n))
            value = jnp.where(code == place, sig - 1.0, sig)
            grad[z * HALF : (z + 1) * HALF, :] = value.astype(BF16)
    slot = lax.broadcasted_iota(jnp.int32, (MOST, ROWS), 0).astype(F32)
    lane = lax.broadcasted_iota(jnp.int32, (HALF, ROWS), 1) // MOST
    for d in range(STEP):
        for hh in range(2):
            pick = jnp.concatenate(
                [
                    jnp.where(
                        jnp.broadcast_to(ranks[d][z : z + 1, :], (MOST, ROWS)) == slot, 1.0, 0.0
                    )
                    for z in range(8 * hh, 8 * hh + 8)
                ],
                axis=0,
            ).astype(BF16)
            mixed = lax.dot_general(
                grad[hh * 512 : (hh + 1) * 512, d * ROWS : (d + 1) * ROWS],
                pick,
                NT,
                preferred_element_type=F32,
            )
            packed = jnp.zeros((HALF, ROWS), F32)
            for z in range(8):
                packed = jnp.where(lane == z, mixed[z * HALF : (z + 1) * HALF, :], packed)
            pack_ref[d, hh * HALF : (hh + 1) * HALF, :] = packed.astype(BF16)


def expert(meta, rows, w):
    count = rows.shape[0]
    return pl.pallas_call(
        expert_body,
        grid_spec=pltpu.PrefetchScalarGridSpec(
            num_scalar_prefetch=1,
            grid=(count // STEP,),
            in_specs=[
                pl.BlockSpec((STEP, ROWS + META, D), lambda i, m: (i, 0, 0)),
                pl.BlockSpec((COLS, D), lambda i, m: (0, 0)),
            ],
            out_specs=[
                pl.BlockSpec((COLS, STEP * ROWS), lambda i, m: (0, i)),
                pl.BlockSpec((STEP, BS, ROWS), lambda i, m: (i, 0, 0)),
            ],
        ),
        out_shape=[
            jax.ShapeDtypeStruct((COLS, count * ROWS), BF16),
            jax.ShapeDtypeStruct((count, BS, ROWS), BF16),
        ],
        compiler_params=pltpu.CompilerParams(vmem_limit_bytes=VMEM),
        cost_estimate=pl.CostEstimate(
            flops=2 * count * ROWS * COLS * D,
            bytes_accessed=10 * 2**20,
            transcendentals=count * ROWS * COLS,
        ),
    )(meta, rows, w)


def weight_body(ga_ref, xa_ref, gb_ref, xb_ref, out_ref, acc):
    step, half = pl.program_id(0), pl.num_programs(0) // 2

    def add(g_ref, x_ref):
        x = x_ref[:, :ROWS, :].reshape(-1, D)
        for q in range(4):
            rows = slice(q * 256, (q + 1) * 256)
            acc[rows, :] += jnp.dot(g_ref[rows, :], x, preferred_element_type=F32)

    @pl.when(step == 0)
    def _():
        acc[...] = jnp.zeros_like(acc)

    @pl.when(step < half)
    def _():
        add(ga_ref, xa_ref)

    @pl.when(step >= half)
    def _():
        add(gb_ref, xb_ref)

    @pl.when(step == pl.num_programs(0) - 1)
    def _():
        out_ref[...] = acc[...].astype(BF16)


def weight_grad(ga, xa, gb, xb):
    count, block = xa.shape[0], 8
    half = count // block
    low = lambda i: jnp.minimum(i, half - 1)
    high = lambda i: jnp.maximum(i - half, 0)
    return pl.pallas_call(
        weight_body,
        grid=(2 * half,),
        in_specs=[
            pl.BlockSpec((COLS, block * ROWS), lambda i: (0, low(i))),
            pl.BlockSpec((block, ROWS + META, D), lambda i: (low(i), 0, 0)),
            pl.BlockSpec((COLS, block * ROWS), lambda i: (0, high(i))),
            pl.BlockSpec((block, ROWS + META, D), lambda i: (high(i), 0, 0)),
        ],
        out_specs=pl.BlockSpec((COLS, D), lambda i: (0, 0)),
        out_shape=jax.ShapeDtypeStruct((COLS, D), BF16),
        scratch_shapes=[pltpu.VMEM((COLS, D), F32)],
        compiler_params=pltpu.CompilerParams(vmem_limit_bytes=VMEM),
        cost_estimate=pl.CostEstimate(
            flops=4 * count * ROWS * COLS * D, bytes_accessed=18 * 2**20, transcendentals=0
        ),
    )(ga, xa, gb, xb)


def row_body(wt_ref, g_ref, out_ref):
    for q in range(D // 256):
        back = jnp.dot(
            wt_ref[q * 256 : (q + 1) * 256, :], g_ref[...], preferred_element_type=F32
        ).astype(BF16)
        for d in range(STEP):
            out_ref[d, q * 256 : (q + 1) * 256, :] = back[:, d * ROWS : (d + 1) * ROWS]


def row_grad(wt, g):
    count = g.shape[1] // ROWS
    return pl.pallas_call(
        row_body,
        grid=(count // STEP,),
        in_specs=[
            pl.BlockSpec((D, COLS), lambda i: (0, 0)),
            pl.BlockSpec((COLS, STEP * ROWS), lambda i: (0, i)),
        ],
        out_specs=pl.BlockSpec((STEP, D, ROWS), lambda i: (i, 0, 0)),
        out_shape=jax.ShapeDtypeStruct((count, D, ROWS), BF16),
        compiler_params=pltpu.CompilerParams(vmem_limit_bytes=VMEM),
        cost_estimate=pl.CostEstimate(
            flops=2 * count * ROWS * COLS * D, bytes_accessed=9 * 2**20, transcendentals=0
        ),
    )(wt, g)


def unpack_body(key_ref, got_ref, out_ref):
    key = key_ref[...]
    lane = lax.broadcasted_iota(jnp.int32, (1, 2 * ROWS), 1)
    total = jnp.zeros(out_ref.shape, F32)
    for owner in range(8):
        for other in range(2):
            chunk = owner * 2 + other
            base = other * BS
            table = jnp.concatenate(
                [
                    jnp.concatenate(
                        [
                            got_ref[2 * owner + h, base + hh * HALF : base + (hh + 1) * HALF, :]
                            for hh in range(2)
                        ],
                        axis=1,
                    )
                    for h in range(2)
                ],
                axis=0,
            )
            pick = jnp.where(key == lane + chunk * 2 * ROWS, 1.0, 0.0).astype(BF16)
            total += lax.dot_general(pick, table, NT, preferred_element_type=F32)
    out_ref[...] = total.astype(BF16)


def unpack(key, got):
    pairs = key.shape[0]
    block = 512
    return pl.pallas_call(
        unpack_body,
        grid=(pairs // block,),
        in_specs=[
            pl.BlockSpec((block, 2 * ROWS), lambda i: (i, 0)),
            pl.BlockSpec(got.shape, lambda i: (0, 0, 0)),
        ],
        out_specs=pl.BlockSpec((block, BS), lambda i: (i, 0)),
        out_shape=jax.ShapeDtypeStruct((pairs, BS), BF16),
        compiler_params=pltpu.CompilerParams(vmem_limit_bytes=VMEM),
        cost_estimate=pl.CostEstimate(
            flops=2 * pairs * 4096 * BS, bytes_accessed=8 * 2**20, transcendentals=0
        ),
    )(key, got)


def shards(features, weights, block_ids, label_codes, counts):
    inst = lax.axis_index(PLANE)
    core = lax.axis_index("core")
    meta = jnp.stack([8 * core + inst // 2, inst % 2]).astype(jnp.int32)
    mine = lax.dynamic_slice_in_dim(weights, inst * HALF, HALF, 0)
    w = lax.all_gather(mine, "z").reshape(COLS, D)

    alive = jnp.arange(TOP, dtype=jnp.int32)[None, :] < counts[:, None]
    code = jnp.where(alive, jnp.minimum(label_codes, BS) + 2, 1)
    slots = jnp.concatenate([block_ids.T, code.T], axis=1).astype(BF16)
    slots = jnp.pad(slots, ((0, 0), (0, D - 2 * ROWS)))
    sent = jnp.concatenate([features, slots], axis=0)
    copies = jnp.broadcast_to(sent[None], (Z,) + sent.shape)
    own = lax.all_to_all(copies, PLANE, split_axis=0, concat_axis=0, tiled=True)
    swap = [(0, 1), (1, 0)]
    own, w = lax.optimization_barrier((own, w))
    wt = w.T
    other = lax.ppermute(own, "core", swap)
    own_grad, own_pack = expert(meta, own, w)
    other_grad, other_pack = expert(meta, other, w)
    other_rows = row_grad(wt, other_grad)
    other_rows, own_grad = lax.optimization_barrier((other_rows, own_grad))
    back_rows = lax.ppermute(other_rows, "core", swap)
    back_pack = lax.ppermute(other_pack, "core", swap)
    total = weight_grad(own_grad, own, other_grad, other)
    total, own_grad = lax.optimization_barrier((total, own_grad))
    grad_w = lax.psum_scatter(
        total.reshape(Z, HALF, D), "z", scatter_dimension=0, tiled=False
    ).astype(F32)
    packs = jnp.concatenate([own_pack, back_pack], axis=1)
    got = lax.all_to_all(packs, PLANE, split_axis=0, concat_axis=0, tiled=True)
    sums = (row_grad(wt, own_grad).astype(F32) + back_rows.astype(F32)).astype(BF16)
    got_rows = lax.all_to_all(sums, PLANE, split_axis=0, concat_axis=0, tiled=True)
    grad_x = jnp.sum(got_rows, axis=0, dtype=F32).T.astype(BF16)

    blocks = jnp.arange(256, dtype=jnp.int32)
    named = (block_ids[:, :, None] == blocks).any(axis=1).astype(BF16)
    order = jnp.arange(ROWS, dtype=jnp.int32)
    before = (order[None, :] < order[:, None]).astype(BF16)
    rank = jnp.dot(before, named, preferred_element_type=F32)
    rank = jnp.sum(jnp.where(block_ids[:, :, None] == blocks, rank[:, None, :], 0.0), axis=2)
    rank = rank.astype(jnp.int32)
    row = block_ids // 16
    owner = block_ids % 16
    crossed = (owner // 8) ^ core
    key = (((owner % 8) * 2 + crossed) * 2 + row // 8) * ROWS + (row % 8) * MOST + rank
    key = jnp.broadcast_to(key.reshape(-1, 1), (ROWS * TOP, 2 * ROWS))
    grad_logits = unpack(key, got).reshape(ROWS, TOP, BS)
    return (grad_x, grad_w, grad_logits)


def solution(mesh):
    mesh = Mesh(mesh.devices.reshape(4, 4, Z, 2), ("y", "x", "z", "core"))
    everywhere = ("y", "x", "z", "core")
    in_specs = (
        P(everywhere, None),
        P(("z", "core"), None),
        P(everywhere, None),
        P(everywhere, None),
        P(everywhere),
    )
    out_specs = (
        P(everywhere, None),
        P(("z", "core", "y", "x"), None),
        P(everywhere, None, None),
    )
    return jax.shard_map(shards, mesh=mesh, in_specs=in_specs, out_specs=out_specs, check_vma=False)
```

```python
import functools

import jax
import jax.numpy as jnp
from jax import lax
from jax.experimental import pallas as pl
from jax.experimental.pallas import tpu as pltpu
from jax.sharding import Mesh
from jax.sharding import PartitionSpec as P

BS = 128
MOST = 16
TOP = 16
ROWS = 128
META = 16
D = 768
Z = 16
HALF = BS // 2
COLS = Z * HALF
STEP = 4
PLANE = ("y", "x")
NT = (((1,), (1,)), ((), ()))
F32 = jnp.float32
BF16 = jnp.bfloat16
VMEM = 48 * 2**20


def expert_body(meta, x_ref, w_ref, grad, pack_ref):
    base = meta[0].astype(F32)
    offset = (meta[1] * HALF + 2).astype(F32)
    n = STEP * ROWS
    x = x_ref[:, :ROWS, :].reshape(n, D)
    local = lax.broadcasted_iota(jnp.int32, (Z, ROWS), 0)
    chunk = (local & 12) + ((local + meta[2]) & 3)
    wanted = chunk.astype(F32) * 16.0 + base
    before = (
        lax.broadcasted_iota(jnp.int32, (ROWS, ROWS), 0)
        < lax.broadcasted_iota(jnp.int32, (ROWS, ROWS), 1)
    ).astype(F32).astype(BF16)
    entries, ranks = [], []
    for d in range(STEP):
        ids = x_ref[d, ROWS : ROWS + TOP, :ROWS].astype(F32)
        codes = x_ref[d, ROWS : ROWS + TOP, ROWS : 2 * ROWS].astype(F32)
        entry = jnp.zeros((Z, ROWS), F32)
        for k in range(TOP):
            entry = entry + jnp.where(ids[k : k + 1, :] == wanted, codes[k : k + 1, :], 0.0)
        named = entry > 0.0
        rank = jnp.dot(
            jnp.where(named, 1.0, 0.0).astype(BF16), before, preferred_element_type=F32
        )
        entries.append(entry)
        ranks.append(jnp.where(named, rank, -1.0))
    entry = jnp.concatenate(entries, axis=1)
    gain = jnp.where(entry >= 2.0, 0.5, 0.0)
    place = lax.broadcasted_iota(jnp.int32, (HALF, n), 0).astype(F32) + offset
    part = 4 * HALF
    for q in range(COLS // part):
        logits = lax.dot_general(
            w_ref[q * part : (q + 1) * part, :], x, NT, preferred_element_type=F32
        )
        for s in range(4):
            z = 4 * q + s
            code = jnp.broadcast_to(entry[z : z + 1, :], (HALF, n))
            own = logits[s * HALF : (s + 1) * HALF, :]
            sig = (jnp.tanh(0.5 * own) + 1.0) * jnp.broadcast_to(gain[z : z + 1, :], (HALF, n))
            value = jnp.where(code == place, sig - 1.0, sig)
            grad[z * HALF : (z + 1) * HALF, :] = value.astype(BF16)
    slot = lax.broadcasted_iota(jnp.int32, (MOST, ROWS), 0).astype(F32)
    lane = lax.broadcasted_iota(jnp.int32, (HALF, ROWS), 1) // MOST
    for d in range(STEP):
        for hh in range(2):
            pick = jnp.concatenate(
                [
                    jnp.where(
                        jnp.broadcast_to(ranks[d][z : z + 1, :], (MOST, ROWS)) == slot, 1.0, 0.0
                    )
                    for z in range(8 * hh, 8 * hh + 8)
                ],
                axis=0,
            ).astype(BF16)
            mixed = lax.dot_general(
                grad[hh * 512 : (hh + 1) * 512, d * ROWS : (d + 1) * ROWS],
                pick,
                NT,
                preferred_element_type=F32,
            )
            packed = jnp.zeros((HALF, ROWS), F32)
            for z in range(8):
                packed = jnp.where(lane == z, mixed[z * HALF : (z + 1) * HALF, :], packed)
            pack_ref[d, hh * HALF : (hh + 1) * HALF, :] = packed.astype(BF16)


def expert(meta, rows, w):
    count = rows.shape[0]
    return pl.pallas_call(
        expert_body,
        grid_spec=pltpu.PrefetchScalarGridSpec(
            num_scalar_prefetch=1,
            grid=(count // STEP,),
            in_specs=[
                pl.BlockSpec((STEP, ROWS + META, D), lambda i, m: (i, 0, 0)),
                pl.BlockSpec((COLS, D), lambda i, m: (0, 0)),
            ],
            out_specs=[
                pl.BlockSpec((COLS, STEP * ROWS), lambda i, m: (0, i)),
                pl.BlockSpec((STEP, BS, ROWS), lambda i, m: (i, 0, 0)),
            ],
        ),
        out_shape=[
            jax.ShapeDtypeStruct((COLS, count * ROWS), BF16),
            jax.ShapeDtypeStruct((count, BS, ROWS), BF16),
        ],
        compiler_params=pltpu.CompilerParams(vmem_limit_bytes=VMEM),
        cost_estimate=pl.CostEstimate(
            flops=2 * count * ROWS * COLS * D,
            bytes_accessed=10 * 2**20,
            transcendentals=count * ROWS * COLS,
        ),
    )(meta, rows, w)


def weight_body(first, *refs):
    if first:
        g_ref, x_ref, out_ref, acc = refs
    else:
        g_ref, x_ref, in_ref, out_ref, acc = refs
    step = pl.program_id(0)

    @pl.when(step == 0)
    def _():
        acc[...] = jnp.zeros_like(acc) if first else in_ref[...]

    x = x_ref[:, :ROWS, :].reshape(-1, D)
    for q in range(4):
        rows = slice(q * 256, (q + 1) * 256)
        acc[rows, :] += jnp.dot(g_ref[rows, :], x, preferred_element_type=F32)

    @pl.when(step == pl.num_programs(0) - 1)
    def _():
        out_ref[...] = acc[...].astype(out_ref.dtype)


def weight_grad(g, x, total=None):
    first = total is None
    count, block = x.shape[0], 8
    whole = pl.BlockSpec((COLS, D), lambda i: (0, 0))
    return pl.pallas_call(
        functools.partial(weight_body, first),
        grid=(count // block,),
        in_specs=[
            pl.BlockSpec((COLS, block * ROWS), lambda i: (0, i)),
            pl.BlockSpec((block, ROWS + META, D), lambda i: (i, 0, 0)),
        ]
        + ([] if first else [whole]),
        out_specs=whole,
        out_shape=jax.ShapeDtypeStruct((COLS, D), F32 if first else BF16),
        scratch_shapes=[pltpu.VMEM((COLS, D), F32)],
        compiler_params=pltpu.CompilerParams(vmem_limit_bytes=VMEM),
        cost_estimate=pl.CostEstimate(
            flops=2 * count * ROWS * COLS * D, bytes_accessed=12 * 2**20, transcendentals=0
        ),
    )(g, x, *([] if first else [total]))


def row_body(first, wt_ref, g_ref, pack_ref, *refs):
    if first:
        (out_ref,) = refs
    else:
        back_ref, out_ref = refs
    for q in range(D // 256):
        rows = slice(q * 256, (q + 1) * 256)
        mine = jnp.dot(wt_ref[rows, :], g_ref[...], preferred_element_type=F32)
        for d in range(STEP):
            part = mine[:, d * ROWS : (d + 1) * ROWS]
            if not first:
                part = part + back_ref[d, rows, :].astype(F32)
            out_ref[d, rows, :] = part.astype(BF16)
    out_ref[:, D : D + BS, :] = pack_ref[...]
    if not first:
        out_ref[:, D + BS :, :] = back_ref[:, D:, :]


def row_grad(wt, g, pack, back=None):
    first = back is None
    count = g.shape[1] // ROWS
    height = D + BS if first else D + 2 * BS
    return pl.pallas_call(
        functools.partial(row_body, first),
        grid=(count // STEP,),
        in_specs=[
            pl.BlockSpec((D, COLS), lambda i: (0, 0)),
            pl.BlockSpec((COLS, STEP * ROWS), lambda i: (0, i)),
            pl.BlockSpec((STEP, BS, ROWS), lambda i: (i, 0, 0)),
        ]
        + ([] if first else [pl.BlockSpec((STEP, D + BS, ROWS), lambda i: (i, 0, 0))]),
        out_specs=pl.BlockSpec((STEP, height, ROWS), lambda i: (i, 0, 0)),
        out_shape=jax.ShapeDtypeStruct((count, height, ROWS), BF16),
        compiler_params=pltpu.CompilerParams(vmem_limit_bytes=VMEM),
        cost_estimate=pl.CostEstimate(
            flops=2 * count * ROWS * COLS * D, bytes_accessed=12 * 2**20, transcendentals=0
        ),
    )(wt, g, pack, *([] if first else [back]))


def finish_body(key_ref, rows_ref, pack_ref, gx_ref, out_ref):
    key = key_ref[...]
    lane = lax.broadcasted_iota(jnp.int32, (1, 2 * ROWS), 1)
    total = jnp.zeros(out_ref.shape, F32)
    for owner in range(8):
        for other in range(2):
            chunk = owner * 2 + other
            base = other * BS
            table = jnp.concatenate(
                [
                    jnp.concatenate(
                        [
                            pack_ref[2 * owner + h, base + hh * HALF : base + (hh + 1) * HALF, :]
                            for hh in range(2)
                        ],
                        axis=1,
                    )
                    for h in range(2)
                ],
                axis=0,
            )
            pick = jnp.where(key == lane + chunk * 2 * ROWS, 1.0, 0.0).astype(BF16)
            total += lax.dot_general(pick, table, NT, preferred_element_type=F32)
    out_ref[...] = total.astype(BF16)
    for q in range(3):
        rows = slice(q * ROWS, (q + 1) * ROWS)
        part = rows_ref[0, rows, :].astype(F32)
        for i in range(1, 16):
            part = part + rows_ref[i, rows, :].astype(F32)
        gx_ref[:, rows] = part.T.astype(BF16)


def finish(key, got):
    pairs, block, deep = key.shape[0], 1024, D // 2
    return pl.pallas_call(
        finish_body,
        grid=(2,),
        in_specs=[
            pl.BlockSpec((block, 2 * ROWS), lambda i: (i, 0)),
            pl.BlockSpec((16, deep, ROWS), lambda i: (0, i, 0)),
            pl.BlockSpec((16, 2 * BS, ROWS), lambda i: (0, 3, 0)),
        ],
        out_specs=[
            pl.BlockSpec((ROWS, deep), lambda i: (0, i)),
            pl.BlockSpec((block, BS), lambda i: (i, 0)),
        ],
        out_shape=[
            jax.ShapeDtypeStruct((ROWS, D), BF16),
            jax.ShapeDtypeStruct((pairs, BS), BF16),
        ],
        compiler_params=pltpu.CompilerParams(vmem_limit_bytes=VMEM),
        cost_estimate=pl.CostEstimate(
            flops=2 * pairs * 4096 * BS, bytes_accessed=8 * 2**20, transcendentals=0
        ),
    )(key, got, got)


def shift(x, k):
    return lax.ppermute(x, ("zhi", "zlo"), [(s, (s - k) % Z) for s in range(Z)])


def gather_z(mine):
    half = HALF // 2
    copies = jnp.broadcast_to(mine[None], (4,) + mine.shape)
    every = lax.all_to_all(copies, "zhi", split_axis=0, concat_axis=0, tiled=True)
    one, last = shift(every, 1), shift(every, -1)
    low, high = shift(every[:, :half], 2), shift(every[:, half:], -2)
    return jnp.stack([every, one, jnp.concatenate([low, high], axis=1), last], axis=1)


def reduce_z(total, after):
    half = HALF // 2
    total = total.reshape(4, 4, HALF, D)
    one, last = shift(total[:, 1], -1), shift(total[:, 3], 1)
    low, high = shift(total[:, 2, :half], -2), shift(total[:, 2, half:], 2)
    every = total[:, 0].astype(F32) + one.astype(F32) + last.astype(F32)
    every = (every + jnp.concatenate([low, high], axis=1).astype(F32)).astype(BF16)
    every, after = lax.optimization_barrier((every, after))
    got = lax.all_to_all(every, "zhi", split_axis=0, concat_axis=0, tiled=True)
    return jnp.sum(got, axis=0, dtype=F32), after


def shards(features, weights, block_ids, label_codes, counts):
    inst = lax.axis_index(PLANE)
    core = lax.axis_index("core")
    depth = lax.axis_index("zlo")
    meta = jnp.stack([8 * core + inst // 2, inst % 2, depth]).astype(jnp.int32)
    mine = lax.dynamic_slice_in_dim(weights, inst * HALF, HALF, 0)
    w = gather_z(mine).reshape(COLS, D)

    alive = jnp.arange(TOP, dtype=jnp.int32)[None, :] < counts[:, None]
    code = jnp.where(alive, jnp.minimum(label_codes, BS) + 2, 1)
    slots = jnp.concatenate([block_ids.T, code.T], axis=1).astype(BF16)
    slots = jnp.pad(slots, ((0, 0), (0, D - 2 * ROWS)))
    sent = jnp.concatenate([features, slots], axis=0)
    copies = jnp.broadcast_to(sent[None], (16,) + sent.shape)
    own = lax.all_to_all(copies, PLANE, split_axis=0, concat_axis=0, tiled=True)
    swap = [(0, 1), (1, 0)]
    own, w = lax.optimization_barrier((own, w))
    wt = w.T
    other = lax.ppermute(own, "core", swap)
    own_grad, own_pack = expert(meta, own, w)
    other, own_grad = lax.optimization_barrier((other, own_grad))
    other_grad, other_pack = expert(meta, other, w)
    other_out = row_grad(wt, other_grad, other_pack)
    back = lax.ppermute(other_out, "core", swap)
    other_out, other_grad = lax.optimization_barrier((other_out, other_grad))
    total = weight_grad(other_grad, other)
    total, own_grad = lax.optimization_barrier((total, own_grad))
    payload = row_grad(wt, own_grad, own_pack, back)
    got = lax.all_to_all(payload, PLANE, split_axis=0, concat_axis=0, tiled=True)
    payload, own_grad = lax.optimization_barrier((payload, own_grad))

    blocks = jnp.arange(256, dtype=jnp.int32)
    named = (block_ids[:, :, None] == blocks).any(axis=1).astype(BF16)
    order = jnp.arange(ROWS, dtype=jnp.int32)
    before = (order[None, :] < order[:, None]).astype(BF16)
    rank = jnp.dot(before, named, preferred_element_type=F32)
    rank = jnp.sum(jnp.where(block_ids[:, :, None] == blocks, rank[:, None, :], 0.0), axis=2)
    rank = rank.astype(jnp.int32)
    row = block_ids // 16
    row = (row & 12) + ((row - depth) & 3)
    owner = block_ids % 16
    crossed = (owner // 8) ^ core
    key = (((owner % 8) * 2 + crossed) * 2 + row // 8) * ROWS + (row % 8) * MOST + rank
    grad_w, key = reduce_z(weight_grad(own_grad, own, total), key)
    key = jnp.broadcast_to(key.reshape(-1, 1), (ROWS * TOP, 2 * ROWS))
    grad_x, grad_logits = finish(key, got)
    grad_logits = grad_logits.reshape(ROWS, TOP, BS)
    return (grad_x, grad_w, grad_logits)


def solution(mesh):
    axes = ("y", "x", "zhi", "zlo", "core")
    mesh = Mesh(mesh.devices.reshape(4, 4, 4, 4, 2), axes)
    in_specs = (
        P(axes, None),
        P(axes[2:], None),
        P(axes, None),
        P(axes, None),
        P(axes),
    )
    out_specs = (
        P(axes, None),
        P(axes[2:] + PLANE, None),
        P(axes, None, None),
    )
    return jax.shard_map(shards, mesh=mesh, in_specs=in_specs, out_specs=out_specs, check_vma=False)
```

```python
import functools

import jax
import jax.numpy as jnp
from jax import lax
from jax.experimental import pallas as pl
from jax.experimental.pallas import tpu as pltpu
from jax.sharding import Mesh
from jax.sharding import PartitionSpec as P

BS = 128
MOST = 16
TOP = 16
ROWS = 128
META = 16
D = 768
Z = 16
HALF = BS // 2
COLS = Z * HALF
STEP = 4
PLANE = ("y", "x")
NT = (((1,), (1,)), ((), ()))
F32 = jnp.float32
BF16 = jnp.bfloat16
VMEM = 48 * 2**20


def expert_body(meta, x_ref, w_ref, grad, pack_ref):
    base = meta[0].astype(F32)
    offset = (meta[1] * HALF + 2).astype(F32)
    n = STEP * ROWS
    x = x_ref[:, :ROWS, :].reshape(n, D)
    wanted = lax.broadcasted_iota(jnp.int32, (Z, ROWS), 0).astype(F32) * 16.0 + base
    before = (
        lax.broadcasted_iota(jnp.int32, (ROWS, ROWS), 0)
        < lax.broadcasted_iota(jnp.int32, (ROWS, ROWS), 1)
    ).astype(F32).astype(BF16)
    entries, ranks = [], []
    for d in range(STEP):
        ids = x_ref[d, ROWS : ROWS + TOP, :ROWS].astype(F32)
        codes = x_ref[d, ROWS : ROWS + TOP, ROWS : 2 * ROWS].astype(F32)
        entry = jnp.zeros((Z, ROWS), F32)
        for k in range(TOP):
            entry = entry + jnp.where(ids[k : k + 1, :] == wanted, codes[k : k + 1, :], 0.0)
        named = entry > 0.0
        rank = jnp.dot(
            jnp.where(named, 1.0, 0.0).astype(BF16), before, preferred_element_type=F32
        )
        entries.append(entry)
        ranks.append(jnp.where(named, rank, -1.0))
    entry = jnp.concatenate(entries, axis=1)
    gain = jnp.where(entry >= 2.0, 0.5, 0.0)
    place = lax.broadcasted_iota(jnp.int32, (HALF, n), 0).astype(F32) + offset
    part = 4 * HALF
    for q in range(COLS // part):
        logits = lax.dot_general(
            w_ref[q * part : (q + 1) * part, :], x, NT, preferred_element_type=F32
        )
        for s in range(4):
            z = 4 * q + s
            code = jnp.broadcast_to(entry[z : z + 1, :], (HALF, n))
            own = logits[s * HALF : (s + 1) * HALF, :]
            sig = (jnp.tanh(0.5 * own) + 1.0) * jnp.broadcast_to(gain[z : z + 1, :], (HALF, n))
            value = jnp.where(code == place, sig - 1.0, sig)
            grad[z * HALF : (z + 1) * HALF, :] = value.astype(BF16)
    slot = lax.broadcasted_iota(jnp.int32, (MOST, ROWS), 0).astype(F32)
    lane = lax.broadcasted_iota(jnp.int32, (HALF, ROWS), 1) // MOST
    for d in range(STEP):
        for hh in range(2):
            pick = jnp.concatenate(
                [
                    jnp.where(
                        jnp.broadcast_to(ranks[d][z : z + 1, :], (MOST, ROWS)) == slot, 1.0, 0.0
                    )
                    for z in range(8 * hh, 8 * hh + 8)
                ],
                axis=0,
            ).astype(BF16)
            mixed = lax.dot_general(
                grad[hh * 512 : (hh + 1) * 512, d * ROWS : (d + 1) * ROWS],
                pick,
                NT,
                preferred_element_type=F32,
            )
            packed = jnp.zeros((HALF, ROWS), F32)
            for z in range(8):
                packed = jnp.where(lane == z, mixed[z * HALF : (z + 1) * HALF, :], packed)
            pack_ref[d, hh * HALF : (hh + 1) * HALF, :] = packed.astype(BF16)


def expert(meta, rows, w):
    count = rows.shape[0]
    return pl.pallas_call(
        expert_body,
        grid_spec=pltpu.PrefetchScalarGridSpec(
            num_scalar_prefetch=1,
            grid=(count // STEP,),
            in_specs=[
                pl.BlockSpec((STEP, ROWS + META, D), lambda i, m: (i, 0, 0)),
                pl.BlockSpec((COLS, D), lambda i, m: (0, 0)),
            ],
            out_specs=[
                pl.BlockSpec((COLS, STEP * ROWS), lambda i, m: (0, i)),
                pl.BlockSpec((STEP, BS, ROWS), lambda i, m: (i, 0, 0)),
            ],
        ),
        out_shape=[
            jax.ShapeDtypeStruct((COLS, count * ROWS), BF16),
            jax.ShapeDtypeStruct((count, BS, ROWS), BF16),
        ],
        compiler_params=pltpu.CompilerParams(vmem_limit_bytes=VMEM),
        cost_estimate=pl.CostEstimate(
            flops=2 * count * ROWS * COLS * D,
            bytes_accessed=10 * 2**20,
            transcendentals=count * ROWS * COLS,
        ),
    )(meta, rows, w)


def weight_body(ga_ref, xa_ref, gb_ref, xb_ref, out_ref, acc):
    step, half = pl.program_id(0), pl.num_programs(0) // 2

    def add(g_ref, x_ref):
        x = x_ref[:, :ROWS, :].reshape(-1, D)
        for q in range(4):
            rows = slice(q * 256, (q + 1) * 256)
            acc[rows, :] += jnp.dot(g_ref[rows, :], x, preferred_element_type=F32)

    @pl.when(step == 0)
    def _():
        acc[...] = jnp.zeros_like(acc)

    @pl.when(step < half)
    def _():
        add(ga_ref, xa_ref)

    @pl.when(step >= half)
    def _():
        add(gb_ref, xb_ref)

    @pl.when(step == pl.num_programs(0) - 1)
    def _():
        out_ref[...] = acc[...].astype(BF16)


def weight_grad(ga, xa, gb, xb):
    count, block = xa.shape[0], 8
    half = count // block
    low = lambda i: jnp.minimum(i, half - 1)
    high = lambda i: jnp.maximum(i - half, 0)
    return pl.pallas_call(
        weight_body,
        grid=(2 * half,),
        in_specs=[
            pl.BlockSpec((COLS, block * ROWS), lambda i: (0, low(i))),
            pl.BlockSpec((block, ROWS + META, D), lambda i: (low(i), 0, 0)),
            pl.BlockSpec((COLS, block * ROWS), lambda i: (0, high(i))),
            pl.BlockSpec((block, ROWS + META, D), lambda i: (high(i), 0, 0)),
        ],
        out_specs=pl.BlockSpec((COLS, D), lambda i: (0, 0)),
        out_shape=jax.ShapeDtypeStruct((COLS, D), BF16),
        scratch_shapes=[pltpu.VMEM((COLS, D), F32)],
        compiler_params=pltpu.CompilerParams(vmem_limit_bytes=VMEM),
        cost_estimate=pl.CostEstimate(
            flops=4 * count * ROWS * COLS * D, bytes_accessed=18 * 2**20, transcendentals=0
        ),
    )(ga, xa, gb, xb)


def row_body(first, wt_ref, g_ref, pack_ref, *refs):
    if first:
        (out_ref,) = refs
    else:
        back_ref, out_ref = refs
    for q in range(D // 256):
        rows = slice(q * 256, (q + 1) * 256)
        mine = jnp.dot(wt_ref[rows, :], g_ref[...], preferred_element_type=F32)
        for d in range(STEP):
            part = mine[:, d * ROWS : (d + 1) * ROWS]
            if not first:
                part = part + back_ref[d, rows, :].astype(F32)
            out_ref[d, rows, :] = part.astype(BF16)
    out_ref[:, D : D + BS, :] = pack_ref[...]
    if not first:
        out_ref[:, D + BS :, :] = back_ref[:, D:, :]


def row_grad(wt, g, pack, back=None):
    first = back is None
    count = g.shape[1] // ROWS
    height = D + BS if first else D + 2 * BS
    return pl.pallas_call(
        functools.partial(row_body, first),
        grid=(count // STEP,),
        in_specs=[
            pl.BlockSpec((D, COLS), lambda i: (0, 0)),
            pl.BlockSpec((COLS, STEP * ROWS), lambda i: (0, i)),
            pl.BlockSpec((STEP, BS, ROWS), lambda i: (i, 0, 0)),
        ]
        + ([] if first else [pl.BlockSpec((STEP, D + BS, ROWS), lambda i: (i, 0, 0))]),
        out_specs=pl.BlockSpec((STEP, height, ROWS), lambda i: (i, 0, 0)),
        out_shape=jax.ShapeDtypeStruct((count, height, ROWS), BF16),
        compiler_params=pltpu.CompilerParams(vmem_limit_bytes=VMEM),
        cost_estimate=pl.CostEstimate(
            flops=2 * count * ROWS * COLS * D, bytes_accessed=12 * 2**20, transcendentals=0
        ),
    )(wt, g, pack, *([] if first else [back]))


def finish_body(key_ref, rows_ref, pack_ref, gx_ref, out_ref):
    key = key_ref[...]
    lane = lax.broadcasted_iota(jnp.int32, (1, 2 * ROWS), 1)
    total = jnp.zeros(out_ref.shape, F32)
    for owner in range(8):
        for other in range(2):
            chunk = owner * 2 + other
            base = other * BS
            table = jnp.concatenate(
                [
                    jnp.concatenate(
                        [
                            pack_ref[2 * owner + h, base + hh * HALF : base + (hh + 1) * HALF, :]
                            for hh in range(2)
                        ],
                        axis=1,
                    )
                    for h in range(2)
                ],
                axis=0,
            )
            pick = jnp.where(key == lane + chunk * 2 * ROWS, 1.0, 0.0).astype(BF16)
            total += lax.dot_general(pick, table, NT, preferred_element_type=F32)
    out_ref[...] = total.astype(BF16)
    for q in range(3):
        rows = slice(q * ROWS, (q + 1) * ROWS)
        part = rows_ref[0, rows, :].astype(F32)
        for i in range(1, 16):
            part = part + rows_ref[i, rows, :].astype(F32)
        gx_ref[:, rows] = part.T.astype(BF16)


def finish(key, got):
    pairs, block, deep = key.shape[0], 1024, D // 2
    return pl.pallas_call(
        finish_body,
        grid=(2,),
        in_specs=[
            pl.BlockSpec((block, 2 * ROWS), lambda i: (i, 0)),
            pl.BlockSpec((16, deep, ROWS), lambda i: (0, i, 0)),
            pl.BlockSpec((16, 2 * BS, ROWS), lambda i: (0, 3, 0)),
        ],
        out_specs=[
            pl.BlockSpec((ROWS, deep), lambda i: (0, i)),
            pl.BlockSpec((block, BS), lambda i: (i, 0)),
        ],
        out_shape=[
            jax.ShapeDtypeStruct((ROWS, D), BF16),
            jax.ShapeDtypeStruct((pairs, BS), BF16),
        ],
        compiler_params=pltpu.CompilerParams(vmem_limit_bytes=VMEM),
        cost_estimate=pl.CostEstimate(
            flops=2 * pairs * 4096 * BS, bytes_accessed=8 * 2**20, transcendentals=0
        ),
    )(key, got, got)


def shards(features, weights, block_ids, label_codes, counts):
    inst = lax.axis_index(PLANE)
    core = lax.axis_index("core")
    meta = jnp.stack([8 * core + inst // 2, inst % 2]).astype(jnp.int32)
    mine = lax.dynamic_slice_in_dim(weights, inst * HALF, HALF, 0)
    mine, features, block_ids = lax.optimization_barrier((mine, features, block_ids))
    w = lax.all_gather(mine, "z").reshape(COLS, D)

    alive = jnp.arange(TOP, dtype=jnp.int32)[None, :] < counts[:, None]
    code = jnp.where(alive, jnp.minimum(label_codes, BS) + 2, 1)
    slots = jnp.concatenate([block_ids.T, code.T], axis=1).astype(BF16)
    slots = jnp.pad(slots, ((0, 0), (0, D - 2 * ROWS)))
    sent = jnp.concatenate([features, slots], axis=0)
    copies = jnp.broadcast_to(sent[None], (16,) + sent.shape)
    own = lax.all_to_all(copies, PLANE, split_axis=0, concat_axis=0, tiled=True)
    swap = [(0, 1), (1, 0)]
    own, w = lax.optimization_barrier((own, w))
    wt = w.T
    other = lax.ppermute(own, "core", swap)
    own_grad, own_pack = expert(meta, own, w)
    other, own_grad = lax.optimization_barrier((other, own_grad))
    other_grad, other_pack = expert(meta, other, w)
    other_out = row_grad(wt, other_grad, other_pack)
    back = lax.ppermute(other_out, "core", swap)
    other_out, own_grad = lax.optimization_barrier((other_out, own_grad))
    total = weight_grad(own_grad, own, other_grad, other)
    total, own_grad = lax.optimization_barrier((total, own_grad))
    grad_w = lax.psum_scatter(
        total.reshape(Z, HALF, D), "z", scatter_dimension=0, tiled=False
    )
    payload = row_grad(wt, own_grad, own_pack, back)
    got = lax.all_to_all(payload, PLANE, split_axis=0, concat_axis=0, tiled=True)

    blocks = jnp.arange(256, dtype=jnp.int32)
    named = (block_ids[:, :, None] == blocks).any(axis=1).astype(BF16)
    order = jnp.arange(ROWS, dtype=jnp.int32)
    before = (order[None, :] < order[:, None]).astype(BF16)
    rank = jnp.dot(before, named, preferred_element_type=F32)
    rank = jnp.sum(jnp.where(block_ids[:, :, None] == blocks, rank[:, None, :], 0.0), axis=2)
    rank = rank.astype(jnp.int32)
    row = block_ids // 16
    owner = block_ids % 16
    crossed = (owner // 8) ^ core
    key = (((owner % 8) * 2 + crossed) * 2 + row // 8) * ROWS + (row % 8) * MOST + rank
    key = jnp.broadcast_to(key.reshape(-1, 1), (ROWS * TOP, 2 * ROWS))
    grad_x, grad_logits = finish(key, got)
    grad_logits = grad_logits.reshape(ROWS, TOP, BS)
    grad_w, grad_x = lax.optimization_barrier((grad_w, grad_x))
    grad_w = grad_w.astype(F32)
    return (grad_x, grad_w, grad_logits)


def solution(mesh):
    mesh = Mesh(mesh.devices.reshape(4, 4, Z, 2), ("y", "x", "z", "core"))
    everywhere = ("y", "x", "z", "core")
    in_specs = (
        P(everywhere, None),
        P(("z", "core"), None),
        P(everywhere, None),
        P(everywhere, None),
        P(everywhere),
    )
    out_specs = (
        P(everywhere, None),
        P(("z", "core", "y", "x"), None),
        P(everywhere, None, None),
    )
    return jax.shard_map(shards, mesh=mesh, in_specs=in_specs, out_specs=out_specs, check_vma=False)
```
